32 devices in a mesh: seq: 8 (over y, x, core), chan: 4 (over z).
Axes of the slice: x: 2, y: 2, z: 4, core: 2. Of those that a mesh axis runs over, the one named last changes fastest.
Arguments:
- token_ids: int32 [4096], P('seq'), may hold values from 0 to 511
- embed_table: bfloat16 [512, 4096], replicated, may hold values from -6 to 6
- in_weight: bfloat16 [4096, 3, 2048], P(None, None, 'chan'), may hold values from -0.09375 to 0.09375
- short_filter: float32 [3, 3, 2048], P(None, None, 'chan'), may hold values from -3 to 3
- long_filter: float32 [4096, 2048], P('seq', 'chan'), may hold values from -1.5 to 1.5
- skip_gain: float32 [2048], P('chan'), may hold values from -4 to 4
- out_weight: bfloat16 [2048, 4096], P('chan'), may hold values from -0.125 to 0.125
Outputs:
- mixed: bfloat16 [4096, 4096], P(('seq', 'chan'))
The draws below stay inside these ranges and needn't reach their ends.
All inputs are finite; a program needn't handle non-finite values.
Results may differ from the reference program's by a relative error of at most 0.0072.
Values may be sent and summed in bfloat16 or wider, within the bound.
A program may use at most 128 MiB of HBM per device.

```python
import math
import jax
import jax.numpy as jnp
import numpy as np

D = 4096
VOCAB = 512
OPERATOR_WIDTH = 2048
TAPS = 3
SEQUENCE_LENGTH = 4096


def draw_long_filter(key, part):
    noise_key = jax.random.fold_in(key, 11)
    rate_key = jax.random.fold_in(key, 12)
    pulse_key = jax.random.fold_in(key, 13)
    delay_positions = jnp.arange(SEQUENCE_LENGTH, dtype=jnp.float32)[:, None]
    log_time = jax.random.uniform(rate_key, (OPERATOR_WIDTH,), jnp.float32, math.log(30.0), math.log(4.0 * SEQUENCE_LENGTH))
    noise_field = jnp.clip(jax.random.normal(noise_key, (SEQUENCE_LENGTH, OPERATOR_WIDTH), jnp.float32), -5.0, 5.0)
    decay_length = jnp.exp(log_time)
    pulse_delays = jax.random.uniform(pulse_key, (3, OPERATOR_WIDTH), jnp.float32, 0.0, 1.0 * SEQUENCE_LENGTH)
    pulse_count = jnp.zeros((SEQUENCE_LENGTH, OPERATOR_WIDTH), jnp.float32)
    for pulse_index in range(3):
        pulse_count = pulse_count + (delay_positions >= pulse_delays[pulse_index][None, :]).astype(jnp.float32)
    envelope = jnp.exp(-delay_positions / decay_length[None, :]) + 0.03
    decay_curve = envelope * jnp.power(0.6, pulse_count)
    scale_factor = 1.0 / jnp.sqrt(jnp.minimum(0.5 * decay_length, 1.0 * SEQUENCE_LENGTH) + 1.0)
    return noise_field * decay_curve * scale_factor[None, :]


def with_ends(result, rng, smallest, largest):
    index_at = [jax.random.randint(jax.random.fold_in(rng, axis), (), 0, length) for axis, length in enumerate(result.shape)]
    main_axis = result.shape.index(max(result.shape))
    next_to = index_at[:main_axis] + [(index_at[main_axis] + 1) % result.shape[main_axis]] + index_at[main_axis + 1:]
    return result.at[tuple(index_at)].set(smallest).at[tuple(next_to)].set(largest)


def block_scale(key, shape, split, smallest, largest):
    factor_of = 1.0
    for position, blocks in split:
        draws = jax.random.uniform(jax.random.fold_in(jax.random.fold_in(key, 6), position), (blocks,), jnp.float32, smallest / len(split), largest / len(split))
        factor_of = factor_of * jnp.repeat(jnp.exp(draws), shape[position] // blocks).reshape((-1,) + (1,) * (len(shape) - 1 - position))
    return factor_of


def rank_bounds(amount, skew):
    weights = [(1 << 20) // math.isqrt(standing ** skew) + 1 for standing in range(1, amount + 1)]
    scale = 1 + sum(weights) // (1 << 30)
    return np.cumsum(np.array([max(1, weight // scale) for weight in weights]))


def skewed_ids(key, extent, number_of, skew):
    grid = rank_bounds(number_of, skew)
    pick = jax.random.randint(jax.random.fold_in(key, 1), extent, 0, int(grid[number_of - 1]))
    rank = jnp.searchsorted(jnp.asarray(grid, jnp.int32), pick, side="right")
    return jax.random.permutation(jax.random.fold_in(key, 2), number_of)[rank].astype(jnp.int32)


def centred(key, shape, width, limit, shards=(), held_as=jnp.bfloat16):
    drawn = width * jax.random.normal(key, shape, jnp.float32)
    if shards:
        drawn = drawn * block_scale(key, shape, shards, -0.22, 0.18)
    return jnp.clip(drawn, -limit, limit).astype(held_as)


def setup_inputs(seed: int = 0) -> dict:
    arg_keys = jax.random.split(jax.random.key(seed), 8)
    token_ids = with_ends(skewed_ids(arg_keys[0], (SEQUENCE_LENGTH,), VOCAB, 2), jax.random.fold_in(arg_keys[0], 3), 0, VOCAB - 1).astype(jnp.int32)
    embed_table = centred(arg_keys[1], (VOCAB, D), 1.0, 6.0)
    in_weight = centred(arg_keys[2], (D, 3, OPERATOR_WIDTH), D ** -0.5, 0.09375, ((2, 4),))
    short_filter = centred(arg_keys[3], (TAPS, 3, OPERATOR_WIDTH), 0.6, 3.0, ((2, 4),), jnp.float32)
    long_filter = draw_long_filter(jax.random.fold_in(arg_keys[7], 71), 0)
    skip_gain = centred(arg_keys[5], (OPERATOR_WIDTH,), 1.0, 4.0, ((0, 4),), jnp.float32)
    out_weight = centred(arg_keys[6], (OPERATOR_WIDTH, D), OPERATOR_WIDTH ** -0.5, 0.125, ((0, 4),))
    return dict(token_ids=token_ids, embed_table=embed_table, in_weight=in_weight, short_filter=short_filter, long_filter=long_filter, skip_gain=skip_gain, out_weight=out_weight)


def reference(token_ids, embed_table, in_weight, short_filter, long_filter, skip_gain, out_weight):
    embedded = jnp.take(embed_table, token_ids, axis=0)
    weights_flat = in_weight.reshape(in_weight.shape[0], -1)
    projected = jnp.dot(embedded, weights_flat, preferred_element_type=jnp.float32).astype(jnp.bfloat16)
    row_count = embedded.shape[0]
    projected = projected.reshape(row_count, 3, -1)
    tap_count = short_filter.shape[0]
    padded = jnp.concatenate([jnp.zeros((tap_count - 1,) + projected.shape[1:], jnp.bfloat16), projected], 0)
    filtered = jnp.zeros(projected.shape, jnp.float32)
    for tap_index in range(tap_count):
        start_row = tap_count - 1 - tap_index
        filtered = filtered + short_filter[tap_index] * padded[start_row:start_row + row_count].astype(jnp.float32)
    gated_value = filtered[:, 0] * filtered[:, 2]
    full_len = 2 * row_count
    spectrum = jnp.fft.rfft(gated_value, n=full_len, axis=0) * jnp.fft.rfft(long_filter, n=full_len, axis=0)
    convolved = jnp.fft.irfft(spectrum, n=full_len, axis=0)[:row_count]
    carried = (filtered[:, 1] * (convolved + skip_gain * gated_value)).astype(jnp.bfloat16)
    return jnp.dot(carried, out_weight, preferred_element_type=jnp.float32).astype(jnp.bfloat16)
```

```python
import functools

import jax
import jax.numpy as jnp
import numpy as np
from jax import lax
from jax.experimental import pallas as pl
from jax.experimental.pallas import tpu as pltpu
from jax.sharding import PartitionSpec as P

HIGHEST = lax.Precision.HIGHEST
LANES = 128
INNER = 64


def transform_matrices(length):
    outer = length // INNER
    n1 = np.arange(outer)[None, :]
    k1 = np.arange(outer)[:, None] + 0.5
    angle = 2.0 * np.pi * n1 * k1 / (2 * outer)
    first = np.concatenate([np.cos(angle), -np.sin(angle)], 0)
    n2 = np.arange(INNER)[None, None, :]
    k2 = np.arange(INNER)[None, :, None]
    turn = 2.0 * np.pi * n2 * (k1[:, :, None] + 2 * outer * k2) / (2 * length)
    cosine, sine = np.cos(turn), -np.sin(turn)
    second = np.concatenate(
        [np.concatenate([cosine, -sine], 2), np.concatenate([sine, cosine], 2)], 1
    )
    last = first.T / length
    return (
        first.astype(np.float32),
        second.astype(np.float32),
        np.swapaxes(second, 1, 2).astype(np.float32),
        last.astype(np.float32),
    )


def dot32(left, right):
    return jnp.dot(left, right, precision=HIGHEST, preferred_element_type=jnp.float32)


def operator_kernel(
    width, ids_ref, table_ref, taps_ref, skip_ref, filter_ref, first_ref, second_ref, back_ref, last_ref,
    out_ref, projected, signal, gate, work
):
    length = ids_ref.shape[0]
    vocab = table_ref.shape[0]
    outer = length // INNER
    chunk = min(512, length)
    tap_count = taps_ref.shape[0] // 3
    projected[pl.ds(0, 8), :] = jnp.zeros((8, projected.shape[1]), jnp.float32)

    @pl.loop(0, length // chunk)
    def _(step):
        start = pl.multiple_of(step * chunk, chunk)
        rows = pl.ds(start, chunk)
        chosen = lax.broadcasted_iota(jnp.int32, (chunk, vocab), 1) == ids_ref[rows, :]
        projected[pl.ds(start + 8, chunk), :] = jnp.dot(
            chosen.astype(jnp.float32).astype(jnp.bfloat16), table_ref[...], preferred_element_type=jnp.float32
        )
        window = projected[pl.ds(start, chunk + 8), :]
        branches = []
        for branch in range(3):
            total = jnp.zeros((chunk, LANES), jnp.float32)
            for tap in range(tap_count):
                part = window[8 - tap : 8 - tap + chunk, branch * LANES : (branch + 1) * LANES]
                row = tap * 3 + branch
                total = total + taps_ref[row : row + 1, :] * part
            branches.append(total)
        gate[rows, :] = branches[1]
        signal[rows, :] = branches[0] * branches[2] + filter_ref[rows, :].astype(jnp.float32)

    @pl.loop(0, INNER, unroll=4)
    def _(n2):
        work[pl.ds(n2 * (2 * outer), 2 * outer), :] = dot32(
            first_ref[...], signal[pl.ds(n2, outer, stride=INNER), :]
        )

    @pl.loop(0, outer, unroll=4)
    def _(k1):
        real_rows = pl.ds(k1, INNER, stride=2 * outer)
        imag_rows = pl.ds(k1 + outer, INNER, stride=2 * outer)
        spectrum = dot32(
            second_ref[k1], jnp.concatenate([work[real_rows, :], work[imag_rows, :]], 0)
        )
        turned = pltpu.roll(spectrum, LANES - width, 1)
        real, imag = spectrum[:INNER], spectrum[INNER:]
        other_real, other_imag = turned[:INNER], turned[INNER:]
        product = jnp.concatenate(
            [real * other_real - imag * other_imag, real * other_imag + imag * other_real], 0
        )
        result = dot32(back_ref[k1], product)
        work[real_rows, :] = result[:INNER]
        work[imag_rows, :] = result[INNER:]

    @pl.loop(0, INNER, unroll=4)
    def _(n2):
        rows = pl.ds(n2, outer, stride=INNER)
        convolved = dot32(last_ref[...], work[pl.ds(n2 * (2 * outer), 2 * outer), :])
        signal[rows, :] = gate[rows, :] * (convolved + skip_ref[0:1, :] * signal[rows, :])

    out_ref[...] = signal[...].astype(jnp.bfloat16)


def run_operator(ids, table, taps, skip, filters, width):
    length = ids.shape[0]
    outer = length // INNER
    matrices = transform_matrices(length)
    spec = pl.BlockSpec(memory_space=pltpu.VMEM)
    return pl.pallas_call(
        functools.partial(operator_kernel, width),
        out_shape=jax.ShapeDtypeStruct((length, LANES), jnp.bfloat16),
        in_specs=[spec] * 9,
        out_specs=spec,
        scratch_shapes=[
            pltpu.VMEM((length + 8, 3 * LANES), jnp.float32),
            pltpu.VMEM((length, LANES), jnp.float32),
            pltpu.VMEM((length, LANES), jnp.float32),
            pltpu.VMEM((2 * length, LANES), jnp.float32),
        ],
        compiler_params=pltpu.CompilerParams(vmem_limit_bytes=60 * 2**20),
        cost_estimate=pl.CostEstimate(flops=10**10, bytes_accessed=2 * 10**7, transcendentals=0),
    )(ids, table, taps, skip, filters, *[jnp.asarray(m) for m in matrices])


def to_lanes(array, before=0):
    pads = [(0, 0)] * (array.ndim - 1) + [(before, LANES - before - array.shape[-1])]
    return jnp.pad(array, pads)


def body(token_ids, embed_table, in_weight, short_filter, long_filter, skip_gain, out_weight):
    place = lax.axis_index("seq")
    seq_count, chan_count = lax.axis_size("seq"), lax.axis_size("chan")
    depth = embed_table.shape[1]
    width = in_weight.shape[2] // seq_count
    columns = out_weight.shape[1] // seq_count

    out_part = lax.dynamic_slice_in_dim(out_weight, place * columns, columns, 1)
    out_all = lax.all_gather(out_part, "chan", axis=0, tiled=False)

    filters = lax.all_to_all(long_filter.astype(jnp.bfloat16), "seq", split_axis=1, concat_axis=0, tiled=True)
    ids = lax.all_gather(token_ids, "seq", axis=0, tiled=True)
    length = ids.shape[0]

    def mine(array):
        return lax.dynamic_slice_in_dim(array, place * width, width, array.ndim - 1)

    table = jnp.einsum(
        "vd,dgc->vgc", embed_table, mine(in_weight), preferred_element_type=jnp.float32
    ).astype(jnp.bfloat16)
    table = to_lanes(table).reshape(embed_table.shape[0], -1)
    taps = to_lanes(mine(short_filter)).reshape(-1, LANES)
    skip = to_lanes(mine(skip_gain)[None])
    carried = run_operator(ids[:, None], table, taps, skip, to_lanes(filters, width), width)[:, :width]

    rows = length // (seq_count * chan_count)
    blocks = carried.reshape(seq_count, chan_count, rows, width)
    blocks = lax.all_to_all(blocks, "chan", split_axis=1, concat_axis=1, tiled=True)
    blocks = blocks.transpose(0, 2, 1, 3).reshape(seq_count * rows, chan_count * width)
    carried_all = lax.all_gather(blocks, "seq", axis=0, tiled=False)
    weight = out_all.reshape(chan_count, seq_count, width, columns).transpose(1, 0, 2, 3)
    weight = weight.reshape(seq_count, chan_count * width, columns)
    mixed = jnp.einsum("stk,skn->tn", carried_all, weight, preferred_element_type=jnp.float32)
    mixed = mixed.astype(jnp.bfloat16).reshape(seq_count, rows, columns)
    mixed = lax.all_to_all(mixed, "seq", split_axis=0, concat_axis=2, tiled=True)
    return mixed[0]


def solution(mesh):
    return jax.shard_map(
        body,
        mesh=mesh,
        in_specs=(
            P("seq"),
            P(),
            P(None, None, "chan"),
            P(None, None, "chan"),
            P("seq", "chan"),
            P("chan"),
            P("chan", None),
        ),
        out_specs=P(("seq", "chan"), None),
        check_vma=False,
    )
```

```python
import functools

import jax
import jax.numpy as jnp
import numpy as np
from jax import lax
from jax.experimental import pallas as pl
from jax.experimental.pallas import tpu as pltpu
from jax.sharding import PartitionSpec as P

LANES = 128
INNER = 64


def transform_matrices(length):
    outer = length // INNER
    n1 = np.arange(outer)[None, :]
    k1 = np.arange(outer)[:, None] + 0.5
    angle = 2.0 * np.pi * n1 * k1 / (2 * outer)
    first = np.concatenate([np.cos(angle), -np.sin(angle)], 0)
    n2 = np.arange(INNER)[None, None, :]
    k2 = np.arange(INNER)[None, :, None]
    turn = 2.0 * np.pi * n2 * (k1[:, :, None] + 2 * outer * k2) / (2 * length)
    cosine, sine = np.cos(turn), -np.sin(turn)
    second = np.concatenate(
        [np.concatenate([cosine, -sine], 2), np.concatenate([sine, cosine], 2)], 1
    )
    last = first.T / length
    return tuple(two_parts(m) for m in (first, second, np.swapaxes(second, 1, 2), last))


def two_parts(matrix):
    high = matrix.astype(jnp.bfloat16)
    low = (matrix - high.astype(np.float64)).astype(jnp.bfloat16)
    return np.concatenate([high, low], -1)


def dot32(left, right):
    high = right.astype(jnp.bfloat16)
    low = (right - high.astype(jnp.float32)).astype(jnp.bfloat16)
    depth = right.shape[0]
    return jnp.dot(left, jnp.concatenate([high, high], 0), preferred_element_type=jnp.float32) + jnp.dot(
        left[:, :depth], low, preferred_element_type=jnp.float32
    )


def operator_kernel(
    width, ids_ref, table_ref, taps_ref, skip_ref, filter_ref, first_ref, second_ref, back_ref, last_ref,
    out_ref, projected, signal, gate, work
):
    length = ids_ref.shape[0]
    vocab = table_ref.shape[0]
    outer = length // INNER
    chunk = min(512, length)
    tap_count = taps_ref.shape[0] // 3
    projected[pl.ds(0, 8), :] = jnp.zeros((8, projected.shape[1]), jnp.float32)

    @pl.loop(0, length // chunk)
    def _(step):
        start = pl.multiple_of(step * chunk, chunk)
        rows = pl.ds(start, chunk)
        chosen = lax.broadcasted_iota(jnp.int32, (chunk, vocab), 1) == ids_ref[rows, :]
        projected[pl.ds(start + 8, chunk), :] = jnp.dot(
            chosen.astype(jnp.float32).astype(jnp.bfloat16), table_ref[...], preferred_element_type=jnp.float32
        )
        window = projected[pl.ds(start, chunk + 8), :]
        branches = []
        for branch in range(3):
            total = jnp.zeros((chunk, LANES), jnp.float32)
            for tap in range(tap_count):
                part = window[8 - tap : 8 - tap + chunk, branch * LANES : (branch + 1) * LANES]
                row = tap * 3 + branch
                total = total + taps_ref[row : row + 1, :] * part
            branches.append(total)
        gate[rows, :] = branches[1]
        signal[rows, :] = branches[0] * branches[2] + filter_ref[rows, :].astype(jnp.float32)

    @pl.loop(0, INNER, unroll=8)
    def _(n2):
        work[pl.ds(n2 * (2 * outer), 2 * outer), :] = dot32(
            first_ref[...], signal[pl.ds(n2, outer, stride=INNER), :]
        )

    @pl.loop(0, outer, unroll=8)
    def _(k1):
        real_rows = pl.ds(k1, INNER, stride=2 * outer)
        imag_rows = pl.ds(k1 + outer, INNER, stride=2 * outer)
        spectrum = dot32(
            second_ref[k1], jnp.concatenate([work[real_rows, :], work[imag_rows, :]], 0)
        )
        turned = pltpu.roll(spectrum, LANES - width, 1)
        real, imag = spectrum[:INNER], spectrum[INNER:]
        other_real, other_imag = turned[:INNER], turned[INNER:]
        product = jnp.concatenate(
            [real * other_real - imag * other_imag, real * other_imag + imag * other_real], 0
        )
        result = dot32(back_ref[k1], product)
        work[real_rows, :] = result[:INNER]
        work[imag_rows, :] = result[INNER:]

    @pl.loop(0, INNER, unroll=8)
    def _(n2):
        rows = pl.ds(n2, outer, stride=INNER)
        convolved = dot32(last_ref[...], work[pl.ds(n2 * (2 * outer), 2 * outer), :])
        signal[rows, :] = gate[rows, :] * (convolved + skip_ref[0:1, :] * signal[rows, :])

    out_ref[...] = signal[...].astype(jnp.bfloat16)


def run_operator(ids, table, taps, skip, filters, width):
    length = ids.shape[0]
    outer = length // INNER
    matrices = transform_matrices(length)
    spec = pl.BlockSpec(memory_space=pltpu.VMEM)
    return pl.pallas_call(
        functools.partial(operator_kernel, width),
        out_shape=jax.ShapeDtypeStruct((length, LANES), jnp.bfloat16),
        in_specs=[spec] * 9,
        out_specs=spec,
        scratch_shapes=[
            pltpu.VMEM((length + 8, 3 * LANES), jnp.float32),
            pltpu.VMEM((length, LANES), jnp.float32),
            pltpu.VMEM((length, LANES), jnp.float32),
            pltpu.VMEM((2 * length, LANES), jnp.float32),
        ],
        compiler_params=pltpu.CompilerParams(vmem_limit_bytes=60 * 2**20),
        cost_estimate=pl.CostEstimate(flops=10**10, bytes_accessed=2 * 10**7, transcendentals=0),
    )(ids, table, taps, skip, filters, *[jnp.asarray(m) for m in matrices])


def to_lanes(array, before=0):
    pads = [(0, 0)] * (array.ndim - 1) + [(before, LANES - before - array.shape[-1])]
    return jnp.pad(array, pads)


def body(token_ids, embed_table, in_weight, short_filter, long_filter, skip_gain, out_weight):
    place = lax.axis_index("seq")
    seq_count, chan_count = lax.axis_size("seq"), lax.axis_size("chan")
    depth = embed_table.shape[1]
    width = in_weight.shape[2] // seq_count
    columns = out_weight.shape[1] // seq_count

    out_part = lax.dynamic_slice_in_dim(out_weight, place * columns, columns, 1)
    out_all = lax.all_gather(out_part, "chan", axis=0, tiled=False)

    digits = jnp.stack([token_ids // 256, token_ids % 256], -1).astype(jnp.bfloat16)
    digits = jnp.broadcast_to(digits[:, None], (digits.shape[0], seq_count, 2))
    sent = long_filter.astype(jnp.bfloat16).reshape(-1, seq_count, width)
    sent = jnp.concatenate([sent, digits], -1)
    received = lax.all_to_all(sent, "seq", split_axis=1, concat_axis=0, tiled=True)[:, 0]
    length = received.shape[0]
    filters = received[:, :width]
    digits = received[:, width:].astype(jnp.int32)
    ids = digits[:, 0] * 256 + digits[:, 1]

    def mine(array):
        return lax.dynamic_slice_in_dim(array, place * width, width, array.ndim - 1)

    table = jnp.einsum(
        "vd,dgc->vgc", embed_table, mine(in_weight), preferred_element_type=jnp.float32
    ).astype(jnp.bfloat16)
    table = to_lanes(table).reshape(embed_table.shape[0], -1)
    taps = to_lanes(mine(short_filter)).reshape(-1, LANES)
    skip = to_lanes(mine(skip_gain)[None])
    carried = run_operator(ids[:, None], table, taps, skip, to_lanes(filters, width), width)[:, :width]

    rows = length // (seq_count * chan_count)
    blocks = carried.reshape(seq_count, chan_count, rows, width)
    blocks = lax.all_to_all(blocks, "chan", split_axis=1, concat_axis=1, tiled=True)
    blocks = blocks.transpose(0, 2, 1, 3).reshape(seq_count * rows, chan_count * width)
    carried_all = lax.all_gather(blocks, "seq", axis=0, tiled=False)
    weight = out_all.reshape(chan_count, seq_count, width, columns).transpose(1, 0, 2, 3)
    weight = weight.reshape(seq_count, chan_count * width, columns)
    mixed = jnp.einsum("stk,skn->tn", carried_all, weight, preferred_element_type=jnp.float32)
    mixed = mixed.astype(jnp.bfloat16).reshape(seq_count, rows, columns)
    mixed = lax.all_to_all(mixed, "seq", split_axis=0, concat_axis=2, tiled=True)
    return mixed[0]


def solution(mesh):
    return jax.shard_map(
        body,
        mesh=mesh,
        in_specs=(
            P("seq"),
            P(),
            P(None, None, "chan"),
            P(None, None, "chan"),
            P("seq", "chan"),
            P("chan"),
            P("chan", None),
        ),
        out_specs=P(("seq", "chan"), None),
        check_vma=False,
    )
```

```python
import functools

import jax
import jax.numpy as jnp
import numpy as np
from jax import lax
from jax.experimental import pallas as pl
from jax.experimental.pallas import tpu as pltpu
from jax.sharding import PartitionSpec as P

LANES = 128
INNER = 64


def transform_matrices(length):
    outer = length // INNER
    n1 = np.arange(outer)[None, :]
    k1 = np.arange(outer)[:, None] + 0.5
    angle = 2.0 * np.pi * n1 * k1 / (2 * outer)
    first = np.concatenate([np.cos(angle), -np.sin(angle)], 0)
    n2 = np.arange(INNER)[None, None, :]
    k2 = np.arange(INNER)[None, :, None]
    turn = 2.0 * np.pi * n2 * (k1[:, :, None] + 2 * outer * k2) / (2 * length)
    cosine, sine = np.cos(turn), -np.sin(turn)
    second = np.concatenate(
        [np.concatenate([cosine, -sine], 2), np.concatenate([sine, cosine], 2)], 1
    )
    last = first.T / length
    return tuple(two_parts(m) for m in (first, second, np.swapaxes(second, 1, 2), last))


def two_parts(matrix):
    high = matrix.astype(jnp.bfloat16)
    low = (matrix - high.astype(np.float64)).astype(jnp.bfloat16)
    return np.concatenate([high, low], -1)


def dot32(left, right):
    high = right.astype(jnp.bfloat16)
    low = (right - high.astype(jnp.float32)).astype(jnp.bfloat16)
    depth = right.shape[0]
    return jnp.dot(left, jnp.concatenate([high, high], 0), preferred_element_type=jnp.float32) + jnp.dot(
        left[:, :depth], low, preferred_element_type=jnp.float32
    )


def operator_kernel(
    width, ids_ref, table_ref, taps_ref, skip_ref, filter_ref, first_ref, second_ref, back_ref, last_ref,
    out_ref, projected, signal, gate, work
):
    length = ids_ref.shape[0]
    vocab = table_ref.shape[0]
    outer = length // INNER
    chunk = min(512, length)
    tap_count = taps_ref.shape[0] // 3
    projected[pl.ds(0, 8), :] = jnp.zeros((8, projected.shape[1]), jnp.float32)

    @pl.loop(0, length // chunk)
    def _(step):
        start = pl.multiple_of(step * chunk, chunk)
        rows = pl.ds(start, chunk)
        chosen = lax.broadcasted_iota(jnp.int32, (chunk, vocab), 1) == ids_ref[rows, :]
        projected[pl.ds(start + 8, chunk), :] = jnp.dot(
            chosen.astype(jnp.float32).astype(jnp.bfloat16), table_ref[...], preferred_element_type=jnp.float32
        )
        window = projected[pl.ds(start, chunk + 8), :]
        branches = []
        for branch in range(3):
            total = jnp.zeros((chunk, LANES), jnp.float32)
            for tap in range(tap_count):
                part = window[8 - tap : 8 - tap + chunk, branch * LANES : (branch + 1) * LANES]
                row = tap * 3 + branch
                total = total + taps_ref[row : row + 1, :] * part
            branches.append(total)
        gate[rows, :] = branches[1]
        signal[rows, :] = branches[0] * branches[2] + filter_ref[rows, :].astype(jnp.float32)

    @pl.loop(0, INNER, unroll=8)
    def _(n2):
        work[pl.ds(n2 * (2 * outer), 2 * outer), :] = dot32(
            first_ref[...], signal[pl.ds(n2, outer, stride=INNER), :]
        )

    @pl.loop(0, outer, unroll=8)
    def _(k1):
        real_rows = pl.ds(k1, INNER, stride=2 * outer)
        imag_rows = pl.ds(k1 + outer, INNER, stride=2 * outer)
        spectrum = dot32(
            second_ref[k1], jnp.concatenate([work[real_rows, :], work[imag_rows, :]], 0)
        )
        turned = pltpu.roll(spectrum, LANES - width, 1)
        real, imag = spectrum[:INNER], spectrum[INNER:]
        other_real, other_imag = turned[:INNER], turned[INNER:]
        product = jnp.concatenate(
            [real * other_real - imag * other_imag, real * other_imag + imag * other_real], 0
        )
        result = dot32(back_ref[k1], product)
        work[real_rows, :] = result[:INNER]
        work[imag_rows, :] = result[INNER:]

    @pl.loop(0, INNER, unroll=8)
    def _(n2):
        rows = pl.ds(n2, outer, stride=INNER)
        convolved = dot32(last_ref[...], work[pl.ds(n2 * (2 * outer), 2 * outer), :])
        signal[rows, :] = gate[rows, :] * (convolved + skip_ref[0:1, :] * signal[rows, :])

    out_ref[...] = signal[...].astype(jnp.bfloat16)


def run_operator(ids, table, taps, skip, filters, width):
    length = ids.shape[0]
    outer = length // INNER
    matrices = transform_matrices(length)
    spec = pl.BlockSpec(memory_space=pltpu.VMEM)
    return pl.pallas_call(
        functools.partial(operator_kernel, width),
        out_shape=jax.ShapeDtypeStruct((length, LANES), jnp.bfloat16),
        in_specs=[spec] * 9,
        out_specs=spec,
        scratch_shapes=[
            pltpu.VMEM((length + 8, 3 * LANES), jnp.float32),
            pltpu.VMEM((length, LANES), jnp.float32),
            pltpu.VMEM((length, LANES), jnp.float32),
            pltpu.VMEM((2 * length, LANES), jnp.float32),
        ],
        compiler_params=pltpu.CompilerParams(vmem_limit_bytes=60 * 2**20),
        cost_estimate=pl.CostEstimate(flops=10**10, bytes_accessed=2 * 10**7, transcendentals=0),
    )(ids, table, taps, skip, filters, *[jnp.asarray(m) for m in matrices])


def to_lanes(array, before=0):
    pads = [(0, 0)] * (array.ndim - 1) + [(before, LANES - before - array.shape[-1])]
    return jnp.pad(array, pads)


def body(token_ids, embed_table, in_weight, short_filter, long_filter, skip_gain, out_weight):
    place = lax.axis_index("seq")
    seq_count, chan_count = lax.axis_size("seq"), lax.axis_size("chan")
    depth = embed_table.shape[1]
    width = in_weight.shape[2] // seq_count
    chips = seq_count // 2
    columns = out_weight.shape[1] // chips
    cores = [[2 * chip, 2 * chip + 1] for chip in range(chips)]
    planes = [[2 * chip + core for chip in range(chips)] for core in range(2)]

    out_part = lax.dynamic_slice_in_dim(out_weight, place * (columns // 2), columns // 2, 1)
    out_part = lax.all_gather(out_part, "chan", axis=0, tiled=False)
    out_all = lax.all_gather(out_part, "seq", axis=0, tiled=False, axis_index_groups=cores)

    digits = jnp.stack([token_ids // 256, token_ids % 256], -1).astype(jnp.bfloat16)
    digits = jnp.broadcast_to(digits[:, None], (digits.shape[0], seq_count, 2))
    sent = long_filter.astype(jnp.bfloat16).reshape(-1, seq_count, width)
    sent = jnp.concatenate([sent, digits], -1)
    received = lax.all_to_all(sent, "seq", split_axis=1, concat_axis=0, tiled=True)[:, 0]
    length = received.shape[0]
    filters = received[:, :width]
    digits = received[:, width:].astype(jnp.int32)
    ids = digits[:, 0] * 256 + digits[:, 1]

    def mine(array):
        return lax.dynamic_slice_in_dim(array, place * width, width, array.ndim - 1)

    table = jnp.einsum(
        "vd,dgc->vgc", embed_table, mine(in_weight), preferred_element_type=jnp.float32
    ).astype(jnp.bfloat16)
    table = to_lanes(table).reshape(embed_table.shape[0], -1)
    taps = to_lanes(mine(short_filter)).reshape(-1, LANES)
    skip = to_lanes(mine(skip_gain)[None])
    carried = run_operator(ids[:, None], table, taps, skip, to_lanes(filters, width), width)[:, :width]

    rows = length // (seq_count * chan_count)
    blocks = carried.reshape(chips, 2, chan_count, rows, width)
    blocks = lax.all_to_all(blocks, "chan", split_axis=2, concat_axis=2, tiled=True)
    blocks = blocks.transpose(1, 0, 3, 2, 4).reshape(2, chips * rows, chan_count * width)
    blocks = lax.all_to_all(
        blocks, "seq", split_axis=0, concat_axis=0, tiled=True, axis_index_groups=cores
    )
    carried_all = lax.all_gather(blocks, "seq", axis=0, tiled=False, axis_index_groups=planes)
    weight = out_all.reshape(2, chan_count, chips, 2, width, columns // 2).transpose(2, 3, 1, 4, 0, 5)
    weight = weight.reshape(chips, 2, chan_count * width, columns)
    mixed = jnp.einsum("pqtk,pqkn->tn", carried_all, weight, preferred_element_type=jnp.float32)
    mixed = mixed.astype(jnp.bfloat16).reshape(chips, rows, columns)
    mixed = lax.all_to_all(
        mixed, "seq", split_axis=0, concat_axis=2, tiled=True, axis_index_groups=planes
    )
    return mixed[0]


def solution(mesh):
    return jax.shard_map(
        body,
        mesh=mesh,
        in_specs=(
            P("seq"),
            P(),
            P(None, None, "chan"),
            P(None, None, "chan"),
            P("seq", "chan"),
            P("chan"),
            P("chan", None),
        ),
        out_specs=P(("seq", "chan"), None),
        check_vma=False,
    )
```

```python
import functools

import jax
import jax.numpy as jnp
import numpy as np
from jax import lax
from jax.experimental import pallas as pl
from jax.experimental.pallas import tpu as pltpu
from jax.sharding import PartitionSpec as P

LANES = 128
INNER = 64


def transform_matrices(length):
    outer = length // INNER
    n1 = np.arange(outer)[None, :]
    k1 = np.arange(outer)[:, None] + 0.5
    angle = 2.0 * np.pi * n1 * k1 / (2 * outer)
    first = np.concatenate([np.cos(angle), -np.sin(angle)], 0)
    n2 = np.arange(INNER)[None, None, :]
    k2 = np.arange(INNER)[None, :, None]
    turn = 2.0 * np.pi * n2 * (k1[:, :, None] + 2 * outer * k2) / (2 * length)
    cosine, sine = np.cos(turn), -np.sin(turn)
    second = np.concatenate(
        [np.concatenate([cosine, -sine], 2), np.concatenate([sine, cosine], 2)], 1
    )
    last = first.T / length
    return tuple(two_parts(m) for m in (first, second, np.swapaxes(second, 1, 2), last))


def two_parts(matrix):
    high = matrix.astype(jnp.bfloat16)
    low = (matrix - high.astype(np.float64)).astype(jnp.bfloat16)
    return np.concatenate([high, low], -1)


def dot32(left, right):
    high = right.astype(jnp.bfloat16)
    low = (right - high.astype(jnp.float32)).astype(jnp.bfloat16)
    depth = right.shape[0]
    return jnp.dot(left, jnp.concatenate([high, high], 0), preferred_element_type=jnp.float32) + jnp.dot(
        left[:, :depth], low, preferred_element_type=jnp.float32
    )


def operator_kernel(
    width, ids_ref, table_ref, taps_ref, skip_ref, filter_ref, first_ref, second_ref, back_ref, last_ref,
    out_ref, projected, signal, gate, work
):
    length = ids_ref.shape[0]
    vocab = table_ref.shape[0]
    outer = length // INNER
    chunk = min(512, length)
    tap_count = taps_ref.shape[0] // 3
    projected[pl.ds(0, 8), :] = jnp.zeros((8, projected.shape[1]), jnp.float32)

    @pl.loop(0, length // chunk)
    def _(step):
        start = pl.multiple_of(step * chunk, chunk)
        rows = pl.ds(start, chunk)
        chosen = lax.broadcasted_iota(jnp.int32, (chunk, vocab), 1) == ids_ref[rows, :]
        projected[pl.ds(start + 8, chunk), :] = jnp.dot(
            chosen.astype(jnp.float32).astype(jnp.bfloat16), table_ref[...], preferred_element_type=jnp.float32
        )
        window = projected[pl.ds(start, chunk + 8), :]
        branches = []
        for branch in range(3):
            total = jnp.zeros((chunk, LANES), jnp.float32)
            for tap in range(tap_count):
                part = window[8 - tap : 8 - tap + chunk, branch * LANES : (branch + 1) * LANES]
                row = tap * 3 + branch
                total = total + taps_ref[row : row + 1, :] * part
            branches.append(total)
        gate[rows, :] = branches[1]
        signal[rows, :] = branches[0] * branches[2] + filter_ref[rows, :].astype(jnp.float32)

    @pl.loop(0, INNER, unroll=8)
    def _(n2):
        work[pl.ds(n2 * (2 * outer), 2 * outer), :] = dot32(
            first_ref[...], signal[pl.ds(n2, outer, stride=INNER), :]
        )

    @pl.loop(0, outer, unroll=8)
    def _(k1):
        real_rows = pl.ds(k1, INNER, stride=2 * outer)
        imag_rows = pl.ds(k1 + outer, INNER, stride=2 * outer)
        spectrum = dot32(
            second_ref[k1], jnp.concatenate([work[real_rows, :], work[imag_rows, :]], 0)
        )
        turned = pltpu.roll(spectrum, LANES - width, 1)
        real, imag = spectrum[:INNER], spectrum[INNER:]
        other_real, other_imag = turned[:INNER], turned[INNER:]
        product = jnp.concatenate(
            [real * other_real - imag * other_imag, real * other_imag + imag * other_real], 0
        )
        result = dot32(back_ref[k1], product)
        work[real_rows, :] = result[:INNER]
        work[imag_rows, :] = result[INNER:]

    @pl.loop(0, INNER, unroll=8)
    def _(n2):
        rows = pl.ds(n2, outer, stride=INNER)
        convolved = dot32(last_ref[...], work[pl.ds(n2 * (2 * outer), 2 * outer), :])
        signal[rows, :] = gate[rows, :] * (convolved + skip_ref[0:1, :] * signal[rows, :])

    out_ref[...] = signal[...].astype(jnp.bfloat16)


def run_operator(ids, table, taps, skip, filters, width):
    length = ids.shape[0]
    outer = length // INNER
    matrices = transform_matrices(length)
    spec = pl.BlockSpec(memory_space=pltpu.VMEM)
    return pl.pallas_call(
        functools.partial(operator_kernel, width),
        out_shape=jax.ShapeDtypeStruct((length, LANES), jnp.bfloat16),
        in_specs=[spec] * 9,
        out_specs=spec,
        scratch_shapes=[
            pltpu.VMEM((length + 8, 3 * LANES), jnp.float32),
            pltpu.VMEM((length, LANES), jnp.float32),
            pltpu.VMEM((length, LANES), jnp.float32),
            pltpu.VMEM((2 * length, LANES), jnp.float32),
        ],
        compiler_params=pltpu.CompilerParams(vmem_limit_bytes=60 * 2**20),
        cost_estimate=pl.CostEstimate(flops=10**10, bytes_accessed=2 * 10**7, transcendentals=0),
    )(ids, table, taps, skip, filters, *[jnp.asarray(m) for m in matrices])


def to_lanes(array, before=0):
    pads = [(0, 0)] * (array.ndim - 1) + [(before, LANES - before - array.shape[-1])]
    return jnp.pad(array, pads)


def body(token_ids, embed_table, in_weight, short_filter, long_filter, skip_gain, out_weight):
    place = lax.axis_index("seq")
    seq_count, chan_count = lax.axis_size("seq"), lax.axis_size("chan")
    depth = embed_table.shape[1]
    width = in_weight.shape[2] // seq_count
    columns = out_weight.shape[1] // seq_count

    out_part = lax.dynamic_slice_in_dim(out_weight, place * columns, columns, 1)
    out_all = lax.all_gather(out_part, "chan", axis=0, tiled=False)

    digits = jnp.stack([token_ids // 256, token_ids % 256], -1).astype(jnp.bfloat16)
    digits = jnp.broadcast_to(digits[:, None], (digits.shape[0], seq_count, 2))
    sent = long_filter.astype(jnp.bfloat16).reshape(-1, seq_count, width)
    sent = jnp.concatenate([sent, digits], -1)
    received = lax.all_to_all(sent, "seq", split_axis=1, concat_axis=0, tiled=True)[:, 0]
    length = received.shape[0]
    filters = received[:, :width]
    digits = received[:, width:].astype(jnp.int32)
    ids = digits[:, 0] * 256 + digits[:, 1]

    def mine(array):
        return lax.dynamic_slice_in_dim(array, place * width, width, array.ndim - 1)

    table = jnp.einsum(
        "vd,dgc->vgc", embed_table, mine(in_weight), preferred_element_type=jnp.float32
    ).astype(jnp.bfloat16)
    table = to_lanes(table).reshape(embed_table.shape[0], -1)
    taps = to_lanes(mine(short_filter)).reshape(-1, LANES)
    skip = to_lanes(mine(skip_gain)[None])
    carried = run_operator(ids[:, None], table, taps, skip, to_lanes(filters, width), width)[:, :width]

    rows = length // (seq_count * chan_count)
    blocks = carried.reshape(seq_count, chan_count, rows, width)
    weight = out_all.reshape(chan_count, seq_count, width, columns).transpose(1, 0, 2, 3)
    weight = weight.reshape(seq_count, chan_count * width, columns)
    half = rows // 2
    results = []
    for part in range(2):
        block = blocks[:, :, part * half : (part + 1) * half]
        block = lax.all_to_all(block, "chan", split_axis=1, concat_axis=1, tiled=True)
        block = block.transpose(0, 2, 1, 3).reshape(seq_count * half, chan_count * width)
        carried_all = lax.all_gather(block, "seq", axis=0, tiled=False)
        mixed = jnp.einsum("stk,skn->tn", carried_all, weight, preferred_element_type=jnp.float32)
        mixed = mixed.astype(jnp.bfloat16).reshape(seq_count, half, columns)
        results.append(lax.all_to_all(mixed, "seq", split_axis=0, concat_axis=2, tiled=True)[0])
    return jnp.concatenate(results, 0)


def solution(mesh):
    return jax.shard_map(
        body,
        mesh=mesh,
        in_specs=(
            P("seq"),
            P(),
            P(None, None, "chan"),
            P(None, None, "chan"),
            P("seq", "chan"),
            P("chan"),
            P("chan", None),
        ),
        out_specs=P(("seq", "chan"), None),
        check_vma=False,
    )
```
